768 devices in a mesh: blk: 32 (over y, x), rep: 24 (over z, core).
Axes of the slice: x: 4, y: 8, z: 12, core: 2. Of those that a mesh axis runs over, the one named last changes fastest.
Arguments:
- features: bfloat16 [393216, 256], P(('blk', 'rep')), may hold values from -6 to 6
- weight: bfloat16 [256, 256], replicated, may hold values from -1.5 to 1.5
- cotangent: bfloat16 [393216, 256], P(('blk', 'rep')), may hold values from -6 to 6
- edge_source: int32 [393216, 16], P(('blk', 'rep')), may hold values from 0 to 3583
- edge_mult: int32 [393216, 16], P(('blk', 'rep')), may hold values from 1 to 4
- read_blocks: int32 [768, 32, 1], P(('blk', 'rep')), may hold values from 0 to 7, as said below
- hub_blocks: int32 [16], replicated, may hold values from 0 to 6143, as said below
Outputs:
- output: bfloat16 [393216, 256], P(('blk', 'rep'))
- feature_grad: float32 [393216, 256], P(('blk', 'rep'))
- weight_grad: float32 [256, 256], replicated
The draws below stay inside these ranges and needn't reach their ends.
Inputs may be any that keep to these rules, and one draw needn't show every extreme that they name: `read_blocks`: for each device and peer the 1 entries are distinct local block indices of that peer. `hub_blocks`: the 16 ids are distinct; block 0 and block 6143 are always among them.
All inputs are finite; a program needn't handle non-finite values.
Results may differ from the reference program's by a relative error of at most 0.015.
Values may be sent and summed in bfloat16 or wider, within the bound.
No kernel may reach another device: no remote copies, remote signals or barrier semaphores. Data moves between devices by JAX's collectives and lax.ppermute only.
A program may use at most 32 MiB of HBM per device.

```python
import jax
import jax.numpy as jnp
from jax import lax

F = 256
BR = 64
BD = 8
K = 16
HUBS = 16
SEND = 1
NODES = 393216
BLOCKS = 6144
TAB = 3584
N_BLK = 32
N_REP = 24


def draw_read_blocks(key, part):
    key = jax.random.fold_in(key, 7)
    count = N_BLK * N_REP * N_BLK
    keys = jax.random.split(key, count)
    picks = jax.vmap(lambda single: jax.random.permutation(single, BD)[:SEND])(keys)
    return picks.reshape(N_BLK * N_REP, N_BLK, SEND).astype(jnp.int32)


def draw_hub_blocks(key, part):
    key = jax.random.fold_in(key, 11)
    middle = jax.random.permutation(key, BLOCKS - 2)[:HUBS - 2].astype(jnp.int32) + 1
    ends = jnp.array([0, BLOCKS - 1], jnp.int32)
    chosen = jnp.concatenate([ends, middle])
    order = jax.random.permutation(jax.random.fold_in(key, 1), HUBS)
    return chosen[order].astype(jnp.int32)


def touch_ends(values, stream_key, least, largest):
    longest = values.shape.index(max(values.shape))
    spots = []
    for shift in (0, 1):
        where = [jax.random.randint(jax.random.fold_in(stream_key, axis), (), 0, length) for axis, length in enumerate(values.shape)]
        where[longest] = (where[longest] + shift) % values.shape[longest]
        spots.append(tuple(where))
    return values.at[spots[0]].set(least).at[spots[1]].set(largest)


def steps_of(stream_key, extent, cuts, low, top_value):
    loudness, own = 1.0, jax.random.fold_in(stream_key, 6)
    for dim, blocks in cuts:
        heights = jnp.exp(jax.random.uniform(jax.random.fold_in(own, dim), (blocks,), jnp.float32, low / len(cuts), top_value / len(cuts)))
        loudness = loudness * jnp.repeat(heights, extent[dim] // blocks).reshape([-1 if axis == dim else 1 for axis in range(len(extent))])
    return loudness


def gaussian(key, dims, spread, most, shards=(), kind=jnp.bfloat16):
    factor_of = steps_of(key, dims, shards, -0.22, 0.18) if shards else 1.0
    values = jax.random.normal(key, dims, jnp.float32) * spread * factor_of
    return jnp.minimum(jnp.maximum(values, -most), most).astype(kind)


def setup_inputs(seed: int = 0) -> dict:
    arg_keys = jax.random.split(jax.random.key(seed), 8)
    return {
        "features": gaussian(arg_keys[0], (NODES, F), 1.0, 6.0, ((0, 768),)),
        "weight": gaussian(arg_keys[1], (F, F), (F // 16) ** -0.5, 1.5),
        "cotangent": gaussian(arg_keys[2], (NODES, F), 1.0, 6.0, ((0, 768),)),
        "edge_source": touch_ends(jax.random.randint(arg_keys[3], (NODES, K), 0, TAB), jax.random.fold_in(arg_keys[3], 1), 0, TAB - 1).astype(jnp.int32),
        "edge_mult": touch_ends(jax.random.randint(arg_keys[4], (NODES, K), 1, 5), jax.random.fold_in(arg_keys[4], 1), 1, 4).astype(jnp.int32),
        "read_blocks": draw_read_blocks(jax.random.fold_in(arg_keys[7], 71), 0),
        "hub_blocks": draw_hub_blocks(jax.random.fold_in(arg_keys[7], 71), 0),
    }


def silu_slope(value):
    sig = jax.nn.sigmoid(value)
    return sig * (1.0 + value * (1.0 - sig))


def source_nodes(read_blocks, hub_blocks):
    devices = N_BLK * N_REP
    per_dev = BD * BR
    device = jnp.arange(devices, dtype=jnp.int32)
    local = device[:, None] * per_dev + jnp.arange(per_dev, dtype=jnp.int32)[None, :]
    hubs = (hub_blocks[:, None] * BR + jnp.arange(BR, dtype=jnp.int32)[None, :]).reshape(-1)
    hubs = jnp.broadcast_to(hubs[None, :], (devices, HUBS * BR))
    rep_index = device % N_REP
    owner = jnp.arange(N_BLK, dtype=jnp.int32)[None, :] * N_REP + rep_index[:, None]
    start = owner[:, :, None] * per_dev + read_blocks * BR
    remote = (start[..., None] + jnp.arange(BR, dtype=jnp.int32)).reshape(devices, N_BLK * SEND * BR)
    return jnp.concatenate([local, hubs, remote], axis=1).astype(jnp.int32)


def reference(features, weight, cotangent, edge_source, edge_mult, read_blocks, hub_blocks):
    devices = N_BLK * N_REP
    per_dev = BD * BR
    table_nodes = source_nodes(read_blocks, hub_blocks)
    mult = edge_mult.astype(jnp.float32)
    edge_weight = mult / jnp.sum(mult, axis=1, keepdims=True)
    source = edge_source.reshape(devices, per_dev, K)
    weights = edge_weight.reshape(devices, per_dev, K)

    def aggregate_one(args):
        nodes, slots, wts = args
        rows = features[nodes[slots]].astype(jnp.float32)
        return jnp.einsum("nk,nkf->nf", wts, rows).astype(jnp.bfloat16)

    aggregated = lax.map(aggregate_one, (table_nodes, source, weights)).reshape(NODES, F)
    pre = jnp.dot(aggregated, weight, preferred_element_type=jnp.float32)
    output = jax.nn.silu(pre).astype(jnp.bfloat16)
    pre_grad = (cotangent.astype(jnp.float32) * silu_slope(pre)).astype(jnp.bfloat16)
    weight_grad = jnp.dot(aggregated.T, pre_grad, preferred_element_type=jnp.float32)
    agg_grad = jnp.dot(pre_grad, weight.T, preferred_element_type=jnp.float32).astype(jnp.bfloat16)
    agg_dev = agg_grad.reshape(devices, per_dev, F)
    limit = per_dev + HUBS * BR
    table_rows = jnp.arange(TAB, dtype=jnp.int32)

    def accumulate(total, args):
        nodes, slots, wts, grads = args
        terms = wts[:, :, None] * grads.astype(jnp.float32)[:, None, :]
        table_grad = jax.ops.segment_sum(terms.reshape(per_dev * K, F), slots.reshape(-1), num_segments=TAB)
        narrow = lax.optimization_barrier(table_grad.astype(jnp.bfloat16))
        rounded = narrow.astype(jnp.float32)
        table_grad = jnp.where((table_rows >= limit)[:, None], rounded, table_grad)
        return total.at[nodes].add(table_grad), None

    feature_grad, _ = lax.scan(accumulate, jnp.zeros((NODES, F), jnp.float32), (table_nodes, source, weights, agg_dev))
    return output, feature_grad, weight_grad
```

```python
import functools

import jax
import jax.numpy as jnp
from jax import lax
from jax.experimental import pallas as pl
from jax.experimental.pallas import tpu as pltpu
from jax.sharding import Mesh, PartitionSpec as P

BR = 64
HALF = BR // 2
GROUP = 16
CHUNK = 24
BF = jnp.bfloat16
F32 = jnp.float32
NT = (((1,), (1,)), ((), ()))
TN = (((0,), (0,)), ((), ()))
VMEM = pl.BlockSpec(memory_space=pltpu.VMEM)
SMEM = pl.BlockSpec(memory_space=pltpu.SMEM)
ANY = pl.BlockSpec(memory_space=pl.ANY)


def call(body, out, in_specs, scratch=(), flops=0, traffic=1 << 20, limit=8, aliases=None):
    several = isinstance(out, (list, tuple))
    return pl.pallas_call(
        body,
        out_shape=out,
        in_specs=in_specs,
        out_specs=[VMEM] * len(out) if several else VMEM,
        scratch_shapes=list(scratch),
        input_output_aliases=aliases or {},
        compiler_params=pltpu.CompilerParams(vmem_limit_bytes=limit << 20),
        cost_estimate=pl.CostEstimate(flops=flops, bytes_accessed=traffic, transcendentals=0),
    )


def build_body(idx_ref, mult_ref, _, m_ref, mt_ref, inv_ref):
    groups, _, lanes = idx_ref.shape
    cols = m_ref.shape[2] // 128
    own = (lax.broadcasted_iota(jnp.int32, (GROUP, lanes), 1) // 16) == lax.broadcasted_iota(
        jnp.int32, (GROUP, lanes), 0
    )
    low = lax.broadcasted_iota(jnp.int32, (128, lanes), 0)

    def group(g, carry):
        idx = idx_ref[g]
        high = idx >> 7
        onehot = jnp.where(low == (idx & 127), 1.0, 0.0).astype(BF)
        mult = jnp.where(own, mult_ref[g].astype(F32), 0.0)
        inv_ref[g] = jnp.broadcast_to(1.0 / jnp.sum(mult, axis=1, keepdims=True), (GROUP, 128))
        left = jnp.concatenate([jnp.where(high == k, mult, 0.0).astype(BF) for k in range(cols)], axis=0)
        dense = lax.dot_general(left, onehot, NT, preferred_element_type=F32).astype(BF)
        for k in range(cols):
            m_ref[g, :, k * 128 : (k + 1) * 128] = dense[k * GROUP : (k + 1) * GROUP]
        return carry

    lax.fori_loop(0, groups, group, 0)
    per = 128 // GROUP

    def turn(k, carry):
        rows = pl.ds(pl.multiple_of(k * 128, 128), 128)
        for n in range(groups // per):
            tile = m_ref[n * per : (n + 1) * per, :, rows].reshape(128, 128)
            mt_ref[rows, n * 128 : (n + 1) * 128] = tile.T
        return carry

    lax.fori_loop(0, cols, turn, 0)


def offer_body(which_ref, wanted_ref, kept_ref, got_ref, out_ref, token_ref):
    rows = kept_ref.shape[0]
    for h in range(out_ref.shape[0] // 2):
        at = which_ref[h]
        inner = jnp.where(at < rows, at, at - rows)
        block = jnp.where(at < rows, kept_ref[inner], got_ref[inner])
        for j in range(2):
            p = 2 * h + j
            out_ref[p, 0:16, :] = block[j * 16 : j * 16 + 16]
            out_ref[p, 16:24, :] = jnp.full((8, out_ref.shape[2]), wanted_ref[p].astype(F32), F32).astype(BF)
    token_ref[...] = jnp.zeros_like(token_ref)


def spread_body(which_ref, source_ref, _, out_ref):
    chosen = source_ref[which_ref[0], 0:16, :]
    for i in range(out_ref.shape[0]):
        out_ref[i] = chosen


def serve_body(which_ref, hub_ref, blocks_ref, pieces_ref, out_ref):
    piece = pieces_ref[hub_ref[0]]
    for i in range(out_ref.shape[0]):
        out_ref[i, 0:BR, :] = blocks_ref[which_ref[i]]
        out_ref[i, BR : BR + 16, :] = piece


def first_body(m_ref, feat_ref, in_ref, acc_ref):
    step = 128
    per_dev, width = feat_ref.shape
    n_half = in_ref.shape[0] * 16
    blocks = in_ref[:, 0:BR, :].reshape(-1, width)
    hubs = in_ref[:, BR : BR + 16, :].reshape(-1, width)

    def rows_of(i, carry):
        rows = pl.ds(pl.multiple_of(i * step, step), step)
        total = jnp.dot(m_ref[rows, 0:per_dev], feat_ref[...], preferred_element_type=F32)
        total += jnp.dot(m_ref[rows, per_dev : per_dev + n_half], hubs, preferred_element_type=F32)
        total += jnp.dot(m_ref[rows, per_dev + 2 * n_half :], blocks, preferred_element_type=F32)
        acc_ref[rows, :] = total
        return carry

    lax.fori_loop(0, per_dev // step, rows_of, 0)


def layer_body(core_ref, acc_ref, m_ref, mt_ref, inv_ref, hub_ref, weight_ref, cot_ref,
               out_ref, gs_ref, keep_ref, send_ref, agg_s, pg_s, w_s):
    step = 128
    per_dev, width = acc_ref.shape
    n_half = hub_ref.shape[0]

    def rows_of(i, carry):
        rows = pl.ds(pl.multiple_of(i * step, step), step)
        total = acc_ref[rows, :] + jnp.dot(
            m_ref[rows, per_dev + n_half : per_dev + 2 * n_half], hub_ref[...], preferred_element_type=F32
        )
        inv = inv_ref[rows, :]
        inv = jnp.concatenate([inv] * (width // 128), axis=1)
        agg = (total * inv).astype(BF)
        agg_s[rows, :] = agg
        pre = jnp.dot(agg, weight_ref[...], preferred_element_type=F32)
        sig = jax.nn.sigmoid(pre)
        out_ref[rows, :] = (pre * sig).astype(BF)
        slope = sig * (1.0 + pre * (1.0 - sig))
        pg = (cot_ref[rows, :].astype(F32) * slope).astype(BF)
        pg_s[rows, :] = pg
        ag = lax.dot_general(pg, weight_ref[...], NT, preferred_element_type=F32).astype(BF)
        gs_ref[rows, :] = (ag.astype(F32) * inv).astype(BF)
        return carry

    lax.fori_loop(0, per_dev // step, rows_of, 0)
    grads = gs_ref[...]
    w_s[...] = lax.dot_general(agg_s[...], pg_s[...], TN, preferred_element_type=F32)
    half = width // 2
    core = core_ref[0]
    for ref, base, part in ((send_ref, per_dev + n_half, 1 - core), (keep_ref, per_dev, core)):
        for k in range(n_half // 256):
            rows = mt_ref[base + k * 256 : base + (k + 1) * 256, :]
            piece = jnp.dot(rows, grads, preferred_element_type=F32).astype(BF)
            ref[k * 16 : (k + 1) * 16, 0:16, :] = piece.reshape(16, 16, width)
        wide = w_s[pl.ds(pl.multiple_of(part * half, half), half), :]
        for d in range(ref.shape[0]):
            tile = wide[(d // 2) * 8 : (d // 2) * 8 + 8, (d % 2) * 128 : (d % 2) * 128 + 128]
            ref[d, 16:24, :] = split(tile)


def table_body(mt_ref, gs_ref, keep_ref, got_ref, local_ref, out_ref):
    grads = gs_ref[...]
    per_dev, width = local_ref.shape
    for k in range(per_dev // 256):
        rows = mt_ref[k * 256 : (k + 1) * 256, :]
        local_ref[k * 256 : (k + 1) * 256, :] = jnp.dot(rows, grads, preferred_element_type=F32)
    peers = out_ref.shape[0]
    first = mt_ref.shape[0] - peers * BR
    per = 256 // BR

    def remote(k, carry):
        rows = pl.ds(pl.multiple_of(first + k * 256, 256), 256)
        piece = jnp.dot(mt_ref[rows, :], grads, preferred_element_type=F32).astype(BF)
        out_ref[pl.ds(k * per, per), 0:BR, :] = piece.reshape(per, BR, width)
        return carry

    lax.fori_loop(0, peers // per, remote, 0)
    for d in range(peers):
        write_chunk(out_ref, (d,), BR, keep_ref[d].astype(F32) + got_ref[d].astype(F32))


def split(wide):
    top = wide.astype(BF)
    rest = (wide - top.astype(F32)).astype(BF)
    return jnp.concatenate([top, rest], axis=1)


def write_chunk(ref, at, first, total):
    ref[at + (slice(first, first + 16), slice(None))] = total[0:16].astype(BF)
    wide = split(total[16:24, 0:128] + total[16:24, 128:256])
    ref[at + (slice(first + 16, first + 24), slice(None))] = wide


def sum_body(first, in_ref, out_ref):
    total = in_ref[0, first : first + CHUNK, :].astype(F32)
    for s in range(1, in_ref.shape[0]):
        total += in_ref[s, first : first + CHUNK, :].astype(F32)
    for d in range(out_ref.shape[0]):
        write_chunk(out_ref, (d,), 0, total)


def gather_body(req_ref, local_ref, back_ref, out_ref):
    out_ref[...] = local_ref[...]

    def one(p, carry):
        out_ref[req_ref[p]] += back_ref[p, 0:BR, :].astype(F32)
        return carry

    lax.fori_loop(0, back_ref.shape[0], one, 0)


def finish_body(meta_ref, acc_ref, mine_ref, other_ref, out_ref, w_ref):
    out_ref[...] = acc_ref[...]
    core = meta_ref[0]
    hubs = mine_ref.shape[0] // 2
    for h in range(hubs):
        block = meta_ref[1 + h]

        @pl.when(block >= 0)
        def _():
            for ref, part in ((mine_ref, core), (other_ref, 1 - core)):
                for j in range(2):
                    rows = pl.ds(pl.multiple_of(part * HALF + j * 16, 16), 16)
                    out_ref[block, rows, :] += ref[2 * h + j, 0:16, :].astype(F32)

    half = w_ref.shape[0] // 2
    for ref, part in ((mine_ref, core), (other_ref, 1 - core)):
        for d in range(ref.shape[0]):
            pair = ref[d, 16:24, :].astype(F32)
            rows = pl.ds(pl.multiple_of(part * half + (d // 2) * 8, 8), 8)
            w_ref[rows, (d % 2) * 128 : (d % 2) * 128 + 128] = pair[:, 0:128] + pair[:, 128:256]


def shards(features, weight, cotangent, edge_source, edge_mult, read_blocks, hub_blocks):
    per_dev, width = features.shape
    blocks_dev = per_dev // BR
    hubs = hub_blocks.shape[0]
    slots = edge_source.shape[1]
    n_blk, n_z = lax.axis_size("blk"), lax.axis_size("z")
    blk, z, core = lax.axis_index("blk"), lax.axis_index("z"), lax.axis_index("core")
    shape = jax.ShapeDtypeStruct
    exchange = functools.partial(lax.all_to_all, split_axis=0, concat_axis=0, tiled=True)
    swap = functools.partial(lax.ppermute, axis_name="core", perm=[(0, 1), (1, 0)])

    hub_device = hub_blocks // blocks_dev
    hub_local = hub_blocks % blocks_dev
    hub_blk = hub_device // (2 * n_z)
    hub_z = (hub_device // 2) % n_z
    hub_core = hub_device % 2
    device = (blk * n_z + z) * 2 + core

    own_blocks = features.reshape(blocks_dev, BR, width)
    wanted = read_blocks.reshape(-1)

    own_halves = own_blocks.reshape(blocks_dev, 2, HALF, width)
    kept = lax.dynamic_index_in_dim(own_halves, core, 1, keepdims=False)
    got = swap(lax.dynamic_index_in_dim(own_halves, 1 - core, 1, keepdims=False))
    where_half = (hub_core ^ core) * blocks_dev + hub_local
    offered, token = call(
        offer_body, [shape((n_blk, CHUNK, width), BF), shape((8, 128), F32)], [SMEM, SMEM, VMEM, VMEM]
    )(where_half, wanted, kept, got)
    pieces = exchange(offered, "blk")

    n_half = hubs * HALF
    hub_row = edge_source - per_dev
    part = ((hub_row // HALF) % 2) ^ core
    moved = per_dev + part * n_half + (hub_row // BR) * HALF + hub_row % HALF
    is_hub = (hub_row >= 0) & (hub_row < 2 * n_half)
    column = jnp.where(is_hub, moved, edge_source)
    groups = per_dev // GROUP
    table_rows = per_dev + 2 * n_half + n_blk * BR
    dense, dense_t, inv = call(
        build_body,
        [
            shape((groups, GROUP, table_rows), BF),
            shape((table_rows, per_dev), BF),
            shape((groups, GROUP, 128), F32),
        ],
        [VMEM, VMEM, VMEM],
        flops=10**10,
        traffic=8 << 20,
        limit=16,
    )(column.reshape(groups, 1, GROUP * slots), edge_mult.reshape(groups, 1, GROUP * slots), token)
    dense = dense.reshape(per_dev, table_rows)
    inv = inv.reshape(per_dev, 128)

    here = blk // 2
    to_z = call(spread_body, shape((n_z, 16, width), BF), [SMEM, VMEM, ANY])(
        lax.dynamic_slice_in_dim(hub_blk, here, 1), pieces, inv
    )
    along = exchange(to_z, "z")
    requested = pieces[:, 16, 0].astype(jnp.int32)
    served = call(serve_body, shape((n_blk, BR + 16, width), BF), [SMEM, SMEM, VMEM, VMEM])(
        requested, lax.dynamic_slice_in_dim(hub_z, here, 1), own_blocks, along
    )
    incoming = exchange(served, "blk")
    hub_other = swap(incoming[:, BR:, :].reshape(-1, width))

    acc = call(
        first_body, shape((per_dev, width), F32), [VMEM] * 3, flops=10**9, traffic=6 << 20, limit=20
    )(dense, features, incoming)
    core_id = core.astype(jnp.int32).reshape(1)
    output, scaled, keep, send = call(
        layer_body,
        [shape((per_dev, width), BF)] * 2 + [shape((n_blk, CHUNK, width), BF)] * 2,
        [SMEM] + [VMEM] * 7,
        scratch=[pltpu.VMEM((per_dev, width), BF)] * 2 + [pltpu.VMEM((width, width), F32)],
        flops=10**9,
        traffic=6 << 20,
        limit=20,
    )(core_id, acc, dense, dense_t, inv, hub_other, weight, cotangent)
    local_grad, grads = call(
        table_body,
        [shape((per_dev, width), F32), shape((n_blk, BR + CHUNK, width), BF)],
        [VMEM] * 4,
        flops=10**9,
        traffic=6 << 20,
        limit=20,
    )(dense_t, scaled, keep, swap(send))

    returned = exchange(grads, "blk")
    chunks = lambda n: shape((n, CHUNK, width), BF)
    by_z = exchange(call(functools.partial(sum_body, BR), chunks(n_z), [VMEM])(returned), "z")
    mine = exchange(call(functools.partial(sum_body, 0), chunks(n_blk), [VMEM])(by_z), "blk")
    other = swap(mine)

    so_far = call(gather_body, shape((blocks_dev, BR, width), F32), [SMEM, VMEM, VMEM], traffic=4 << 20)(
        requested, local_grad.reshape(blocks_dev, BR, width), returned
    )
    meta = jnp.concatenate([core_id, jnp.where(hub_device == device, hub_local, -1).astype(jnp.int32)])
    feature_grad, weight_grad = call(
        finish_body,
        [shape((blocks_dev, BR, width), F32), shape((width, width), F32)],
        [SMEM] + [VMEM] * 3,
    )(meta, so_far, mine, other)
    return output, feature_grad.reshape(per_dev, width), weight_grad


def solution(mesh):
    n_blk, n_rep = mesh.devices.shape
    fine = Mesh(mesh.devices.reshape(n_blk, n_rep // 2, 2), ("blk", "z", "core"))
    axes = ("blk", "z", "core")
    rows = P(axes, None)
    in_specs = (rows, P(), rows, rows, rows, P(axes, None, None), P())
    out_specs = (rows, rows, P())
    return jax.shard_map(shards, mesh=fine, in_specs=in_specs, out_specs=out_specs, check_vma=False)
```

```python
import functools

import jax
import jax.numpy as jnp
from jax import lax
from jax.experimental import pallas as pl
from jax.experimental.pallas import tpu as pltpu
from jax.sharding import Mesh, PartitionSpec as P

BR = 64
PER_DEV = 512
HALF = BR // 2
GROUP = 16
CHUNK = 24
BF = jnp.bfloat16
F32 = jnp.float32
NT = (((1,), (1,)), ((), ()))
TN = (((0,), (0,)), ((), ()))
VMEM = pl.BlockSpec(memory_space=pltpu.VMEM)
SMEM = pl.BlockSpec(memory_space=pltpu.SMEM)
ANY = pl.BlockSpec(memory_space=pl.ANY)


def call(body, out, in_specs, scratch=(), flops=0, traffic=1 << 20, limit=8, outs=None):
    several = isinstance(out, (list, tuple))
    out_specs = outs or ([VMEM] * len(out) if several else VMEM)
    return pl.pallas_call(
        body,
        out_shape=out,
        in_specs=in_specs,
        out_specs=out_specs,
        scratch_shapes=list(scratch),
        compiler_params=pltpu.CompilerParams(vmem_limit_bytes=limit << 20),
        cost_estimate=pl.CostEstimate(flops=flops, bytes_accessed=traffic, transcendentals=0),
    )


def build_body(core_ref, idx_ref, mult_ref, main_ref, hub_ref, inv_ref, main_s, sems):
    groups, _, lanes = idx_ref.shape
    hub_cols = hub_ref.shape[2] // 128
    cols = main_ref.shape[2] // 128 + hub_cols
    first = PER_DEV // 128
    n_half = hub_cols * 64
    core = core_ref[0]
    own = (lax.broadcasted_iota(jnp.int32, (GROUP, lanes), 1) // 16) == lax.broadcasted_iota(
        jnp.int32, (GROUP, lanes), 0
    )
    low = lax.broadcasted_iota(jnp.int32, (128, lanes), 0)

    def group(g, carry):
        idx = idx_ref[g]
        row = idx - PER_DEV
        moved = PER_DEV + (((row >> 5) & 1) ^ core) * n_half + (row >> 6) * HALF + (row & (HALF - 1))
        idx = jnp.where((row >= 0) & (row < 2 * n_half), moved, idx)
        high = idx >> 7
        onehot = jnp.where(low == (idx & 127), 1.0, 0.0).astype(BF)
        mult = jnp.where(own, mult_ref[g].astype(F32), 0.0)
        inv_ref[g] = jnp.broadcast_to(1.0 / jnp.sum(mult, axis=1, keepdims=True), (GROUP, 128))
        left = jnp.concatenate([jnp.where(high == k, mult, 0.0).astype(BF) for k in range(cols)], axis=0)
        dense = lax.dot_general(left, onehot, NT, preferred_element_type=F32).astype(BF)
        for k in range(cols):
            tile = dense[k * GROUP : (k + 1) * GROUP]
            if first <= k < first + hub_cols:
                hub_ref[g, :, (k - first) * 128 : (k - first + 1) * 128] = tile
            else:
                at = k if k < first else k - hub_cols
                main_s[g, :, at * 128 : (at + 1) * 128] = tile
        return carry

    parts = sems.shape[0]
    per = groups // parts
    copies = []
    for q in range(parts):
        lax.fori_loop(q * per, (q + 1) * per, group, 0, unroll=4)
        rows = pl.ds(q * per, per)
        copies.append(pltpu.make_async_copy(main_s.at[rows], main_ref.at[rows], sems.at[q]))
        copies[-1].start()
    for copy in copies:
        copy.wait()


def offer_body(which_ref, wanted_ref, kept_ref, got_ref, out_ref):
    rows = kept_ref.shape[0]
    for h in range(out_ref.shape[0] // 2):
        at = which_ref[h]
        inner = jnp.where(at < rows, at, at - rows)
        block = jnp.where(at < rows, kept_ref[inner], got_ref[inner])
        for j in range(2):
            p = 2 * h + j
            out_ref[p, 0:16, :] = block[j * 16 : j * 16 + 16]
            out_ref[p, 16:24, :] = jnp.full((8, out_ref.shape[2]), wanted_ref[p].astype(F32), F32).astype(BF)


def pick_body(which_ref, here_ref, hub_blk_ref, blocks_ref, pieces_ref, _, out_ref, piece_ref):
    piece_ref[...] = pieces_ref[hub_blk_ref[here_ref[0]], 0:16, :]
    for i in range(out_ref.shape[0]):
        out_ref[i] = blocks_ref[which_ref[i]]


def spread_body(here_ref, hub_z_ref, source_ref, _, out_ref):
    chosen = source_ref[hub_z_ref[here_ref[0]]]
    for i in range(out_ref.shape[0]):
        out_ref[i] = chosen


def first_body(m_ref, feat_ref, in_ref, _, acc_ref):
    step = 128
    per_dev = feat_ref.shape[0]
    first = m_ref.shape[1] - in_ref.shape[0]

    def rows_of(i, carry):
        rows = pl.ds(pl.multiple_of(i * step, step), step)
        total = jnp.dot(m_ref[rows, 0:per_dev], feat_ref[...], preferred_element_type=F32)
        total += jnp.dot(m_ref[rows, first:], in_ref[...], preferred_element_type=F32)
        acc_ref[rows, :] = total
        return carry

    lax.fori_loop(0, per_dev // step, rows_of, 0)


def layer_body(core_ref, acc_ref, m_ref, inv_ref, mine_ref, other_ref, weight_ref, cot_ref,
               out_ref, gs_ref, keep_ref, send_ref, agg_s, pg_s, w_s):
    step = 128
    per_dev, width = acc_ref.shape
    n_half = mine_ref.shape[0]

    def rows_of(i, carry):
        rows = pl.ds(pl.multiple_of(i * step, step), step)
        total = acc_ref[rows, :]
        for base, ref in ((0, mine_ref), (n_half, other_ref)):
            total += jnp.dot(m_ref[rows, base : base + n_half], ref[...], preferred_element_type=F32)
        inv = inv_ref[rows, :]
        inv = jnp.concatenate([inv] * (width // 128), axis=1)
        agg = (total * inv).astype(BF)
        agg_s[rows, :] = agg
        pre = jnp.dot(agg, weight_ref[...], preferred_element_type=F32)
        sig = jax.nn.sigmoid(pre)
        out_ref[rows, :] = (pre * sig).astype(BF)
        slope = sig * (1.0 + pre * (1.0 - sig))
        pg = (cot_ref[rows, :].astype(F32) * slope).astype(BF)
        pg_s[rows, :] = pg
        ag = lax.dot_general(pg, weight_ref[...], NT, preferred_element_type=F32).astype(BF)
        gs_ref[rows, :] = (ag.astype(F32) * inv).astype(BF)
        return carry

    lax.fori_loop(0, per_dev // step, rows_of, 0)
    grads = gs_ref[...]
    w_s[...] = lax.dot_general(agg_s[...], pg_s[...], TN, preferred_element_type=F32)
    half = width // 2
    core = core_ref[0]
    for ref, base, part in ((send_ref, n_half, 1 - core), (keep_ref, 0, core)):
        for k in range(n_half // 256):
            cols = m_ref[:, base + k * 256 : base + (k + 1) * 256]
            piece = lax.dot_general(cols, grads, TN, preferred_element_type=F32).astype(BF)
            ref[k * 16 : (k + 1) * 16, 0:16, :] = piece.reshape(16, 16, width)
        wide = w_s[pl.ds(pl.multiple_of(part * half, half), half), :]
        for d in range(ref.shape[0]):
            tile = wide[(d // 2) * 8 : (d // 2) * 8 + 8, (d % 2) * 128 : (d % 2) * 128 + 128]
            ref[d, 16:24, :] = split(tile)


def table_body(m_ref, gs_ref, local_ref, remote_ref):
    grads = gs_ref[...]
    per_dev = local_ref.shape[0]
    for k in range(m_ref.shape[1] // 256):
        rows = slice(k * 256, (k + 1) * 256)
        piece = lax.dot_general(m_ref[:, rows], grads, TN, preferred_element_type=F32)
        if k < per_dev // 256:
            local_ref[rows, :] = piece
        else:
            remote_ref[k * 256 - per_dev : (k + 1) * 256 - per_dev, :] = piece.astype(BF)


def split(wide):
    top = wide.astype(BF)
    rest = (wide - top.astype(F32)).astype(BF)
    return jnp.concatenate([top, rest], axis=1)


def write_chunk(ref, at, total):
    ref[at + (slice(0, 16), slice(None))] = total[0:16].astype(BF)
    ref[at + (slice(16, 24), slice(None))] = split(total[16:24, 0:128] + total[16:24, 128:256])


def pair_body(keep_ref, got_ref, out_ref):
    for d in range(out_ref.shape[0]):
        write_chunk(out_ref, (d,), keep_ref[d].astype(F32) + got_ref[d].astype(F32))


def sum_body(in_ref, *refs):
    out_ref = refs[-1]
    total = in_ref[0].astype(F32)
    for s in range(1, in_ref.shape[0]):
        total += in_ref[s].astype(F32)
    if len(out_ref.shape) == 2:
        write_chunk(out_ref, (), total)
    else:
        for d in range(out_ref.shape[0]):
            write_chunk(out_ref, (d,), total)


def alias_body(*refs):
    pass


def copy_body(value_ref, _, out_ref):
    out_ref[...] = value_ref[...]


def gather_body(req_ref, local_ref, back_ref, out_ref):
    out_ref[...] = local_ref[...]

    def one(p, carry):
        out_ref[req_ref[p]] += back_ref[p].astype(F32)
        return carry

    lax.fori_loop(0, back_ref.shape[0], one, 0)


def finish_body(meta_ref, acc_ref, mine_ref, other_ref, out_ref, w_ref):
    out_ref[...] = acc_ref[...]
    core = meta_ref[0]
    hubs = mine_ref.shape[0] // 2
    for h in range(hubs):
        block = meta_ref[1 + h]

        @pl.when(block >= 0)
        def _():
            for ref, part in ((mine_ref, core), (other_ref, 1 - core)):
                for j in range(2):
                    rows = pl.ds(pl.multiple_of(part * HALF + j * 16, 16), 16)
                    out_ref[block, rows, :] += ref[2 * h + j, 0:16, :].astype(F32)

    half = w_ref.shape[0] // 2
    for ref, part in ((mine_ref, core), (other_ref, 1 - core)):
        for d in range(ref.shape[0]):
            pair = ref[d, 16:24, :].astype(F32)
            rows = pl.ds(pl.multiple_of(part * half + (d // 2) * 8, 8), 8)
            w_ref[rows, (d % 2) * 128 : (d % 2) * 128 + 128] = pair[:, 0:128] + pair[:, 128:256]


def shards(features, weight, cotangent, edge_source, edge_mult, read_blocks, hub_blocks):
    per_dev, width = features.shape
    blocks_dev = per_dev // BR
    hubs = hub_blocks.shape[0]
    slots = edge_source.shape[1]
    n_blk, n_z = lax.axis_size("blk"), lax.axis_size("z")
    blk, z, core = lax.axis_index("blk"), lax.axis_index("z"), lax.axis_index("core")
    shape = jax.ShapeDtypeStruct
    exchange = functools.partial(lax.all_to_all, split_axis=0, concat_axis=0, tiled=True)
    swap = functools.partial(lax.ppermute, axis_name="core", perm=[(0, 1), (1, 0)])

    hub_device = hub_blocks // blocks_dev
    hub_local = hub_blocks % blocks_dev
    hub_blk = hub_device // (2 * n_z)
    hub_z = (hub_device // 2) % n_z
    hub_core = hub_device % 2
    device = (blk * n_z + z) * 2 + core

    own_blocks = features.reshape(blocks_dev, BR, width)
    wanted = read_blocks.reshape(-1)

    own_halves = own_blocks.reshape(blocks_dev, 2, HALF, width)
    kept = lax.dynamic_index_in_dim(own_halves, core, 1, keepdims=False)
    got = swap(lax.dynamic_index_in_dim(own_halves, 1 - core, 1, keepdims=False))
    where_half = (hub_core ^ core) * blocks_dev + hub_local
    offered = call(
        offer_body, shape((n_blk, CHUNK, width), BF), [SMEM, SMEM, VMEM, VMEM]
    )(where_half, wanted, kept, got)
    pieces = exchange(offered, "blk")

    n_half = hubs * HALF
    core_id = core.astype(jnp.int32).reshape(1)
    groups = per_dev // GROUP
    main_rows = per_dev + n_blk * BR
    main, dense_hub, inv = call(
        build_body,
        [
            shape((groups, GROUP, main_rows), BF),
            shape((groups, GROUP, 2 * n_half), BF),
            shape((groups, GROUP, 128), F32),
        ],
        [SMEM, VMEM, VMEM],
        scratch=[pltpu.VMEM((groups, GROUP, main_rows), BF), pltpu.SemaphoreType.DMA((4,))],
        flops=8 * 10**9,
        traffic=8 << 20,
        limit=16,
        outs=[pl.BlockSpec(memory_space=pltpu.HBM), VMEM, VMEM],
    )(core_id, edge_source.reshape(groups, 1, GROUP * slots), edge_mult.reshape(groups, 1, GROUP * slots))
    main = main.reshape(per_dev, main_rows)
    dense_hub = dense_hub.reshape(per_dev, 2 * n_half)
    inv = inv.reshape(per_dev, 128)

    here = (blk // 2).astype(jnp.int32).reshape(1)
    requested = pieces[:, 16, 0].astype(jnp.int32)
    outgoing, piece = call(
        pick_body,
        [shape((n_blk, BR, width), BF), shape((16, width), BF)],
        [SMEM] * 3 + [VMEM] * 2 + [ANY],
    )(requested, here, hub_blk, own_blocks, pieces, inv)
    incoming = exchange(outgoing, "blk").reshape(-1, width)
    along = lax.all_gather(piece, "z")
    to_blk = call(spread_body, shape((n_blk, 16, width), BF), [SMEM, SMEM, VMEM, ANY])(
        here, hub_z, along, incoming
    )
    acc = call(
        first_body, shape((per_dev, width), F32), [VMEM] * 3 + [ANY], flops=10**9, traffic=6 << 20, limit=20
    )(main, features, incoming, to_blk)
    hub_mine = call(copy_body, shape((hubs * HALF, width), BF), [VMEM, VMEM])(
        exchange(to_blk, "blk").reshape(-1, width), acc
    )
    hub_other = swap(hub_mine)

    output, scaled, keep, send = call(
        layer_body,
        [shape((per_dev, width), BF)] * 2 + [shape((n_blk, CHUNK, width), BF)] * 2,
        [SMEM] + [VMEM] * 7,
        scratch=[pltpu.VMEM((per_dev, width), BF)] * 2 + [pltpu.VMEM((width, width), F32)],
        flops=10**9,
        traffic=6 << 20,
        limit=20,
    )(core_id, acc, dense_hub, inv, hub_mine, hub_other, weight, cotangent)
    local_grad, remote_grad = call(
        table_body,
        [shape((per_dev, width), F32), shape((n_blk * BR, width), BF)],
        [VMEM, VMEM],
        flops=10**9,
        traffic=6 << 20,
        limit=20,
    )(main, scaled)

    chunk = shape((CHUNK, width), BF)
    chunks = shape((n_blk, CHUNK, width), BF)
    by_blk = exchange(call(pair_body, chunks, [VMEM, VMEM])(keep, swap(send)), "blk")
    part_sum = call(sum_body, chunk, [VMEM])(by_blk)
    remote_grad = pl.pallas_call(
        alias_body,
        out_shape=shape(remote_grad.shape, BF),
        in_specs=[ANY, VMEM],
        out_specs=ANY,
        input_output_aliases={0: 0},
    )(remote_grad, part_sum)
    returned = exchange(remote_grad.reshape(n_blk, BR, width), "blk")
    full_sum = call(sum_body, chunks, [VMEM, ANY])(lax.all_gather(part_sum, "z"), returned)
    mine = exchange(full_sum, "blk")
    other = swap(mine)

    so_far = call(gather_body, shape((blocks_dev, BR, width), F32), [SMEM, VMEM, VMEM], traffic=4 << 20)(
        requested, local_grad.reshape(blocks_dev, BR, width), returned
    )
    meta = jnp.concatenate([core_id, jnp.where(hub_device == device, hub_local, -1).astype(jnp.int32)])
    feature_grad, weight_grad = call(
        finish_body,
        [shape((blocks_dev, BR, width), F32), shape((width, width), F32)],
        [SMEM] + [VMEM] * 3,
    )(meta, so_far, mine, other)
    return output, feature_grad.reshape(per_dev, width), weight_grad


def solution(mesh):
    n_blk, n_rep = mesh.devices.shape
    fine = Mesh(mesh.devices.reshape(n_blk, n_rep // 2, 2), ("blk", "z", "core"))
    axes = ("blk", "z", "core")
    rows = P(axes, None)
    in_specs = (rows, P(), rows, rows, rows, P(axes, None, None), P())
    out_specs = (rows, rows, P())
    return jax.shard_map(shards, mesh=fine, in_specs=in_specs, out_specs=out_specs, check_vma=False)
```

```python
import functools

import jax
import jax.numpy as jnp
from jax import lax
from jax.experimental import pallas as pl
from jax.experimental.pallas import tpu as pltpu
from jax.sharding import Mesh, PartitionSpec as P

BR = 64
PER_DEV = 512
HALF = BR // 2
GROUP = 16
CHUNK = 40
BF = jnp.bfloat16
F32 = jnp.float32
NT = (((1,), (1,)), ((), ()))
TN = (((0,), (0,)), ((), ()))
VMEM = pl.BlockSpec(memory_space=pltpu.VMEM)
SMEM = pl.BlockSpec(memory_space=pltpu.SMEM)
ANY = pl.BlockSpec(memory_space=pl.ANY)


def call(body, out, in_specs, scratch=(), flops=0, traffic=1 << 20, limit=8, outs=None):
    several = isinstance(out, (list, tuple))
    out_specs = outs or ([VMEM] * len(out) if several else VMEM)
    return pl.pallas_call(
        body,
        out_shape=out,
        in_specs=in_specs,
        out_specs=out_specs,
        scratch_shapes=list(scratch),
        compiler_params=pltpu.CompilerParams(vmem_limit_bytes=limit << 20),
        cost_estimate=pl.CostEstimate(flops=flops, bytes_accessed=traffic, transcendentals=0),
    )


def build_body(core_ref, idx_ref, mult_ref, main_ref, hub_ref, inv_ref, main_s, sems):
    groups, _, lanes = idx_ref.shape
    hub_cols = hub_ref.shape[2] // 128
    cols = main_ref.shape[2] // 128 + hub_cols
    first = PER_DEV // 128
    n_half = hub_cols * 64
    core = core_ref[0]
    own = (lax.broadcasted_iota(jnp.int32, (GROUP, lanes), 1) // 16) == lax.broadcasted_iota(
        jnp.int32, (GROUP, lanes), 0
    )
    low = lax.broadcasted_iota(jnp.int32, (128, lanes), 0)

    def group(g, carry):
        idx = idx_ref[g]
        row = idx - PER_DEV
        moved = PER_DEV + (((row >> 5) & 1) ^ core) * n_half + (row >> 6) * HALF + (row & (HALF - 1))
        idx = jnp.where((row >= 0) & (row < 2 * n_half), moved, idx)
        high = idx >> 7
        onehot = jnp.where(low == (idx & 127), 1.0, 0.0).astype(BF)
        mult = jnp.where(own, mult_ref[g].astype(F32), 0.0)
        inv_ref[g] = jnp.broadcast_to(1.0 / jnp.sum(mult, axis=1, keepdims=True), (GROUP, 128))
        left = jnp.concatenate([jnp.where(high == k, mult, 0.0).astype(BF) for k in range(cols)], axis=0)
        dense = lax.dot_general(left, onehot, NT, preferred_element_type=F32).astype(BF)
        for k in range(cols):
            tile = dense[k * GROUP : (k + 1) * GROUP]
            if first <= k < first + hub_cols:
                hub_ref[g, :, (k - first) * 128 : (k - first + 1) * 128] = tile
            else:
                at = k if k < first else k - hub_cols
                main_s[g, :, at * 128 : (at + 1) * 128] = tile
        return carry

    parts = sems.shape[0]
    per = groups // parts
    copies = []
    for q in range(parts):
        lax.fori_loop(q * per, (q + 1) * per, group, 0, unroll=4)
        rows = pl.ds(q * per, per)
        copies.append(pltpu.make_async_copy(main_s.at[rows], main_ref.at[rows], sems.at[q]))
        copies[-1].start()
    for copy in copies:
        copy.wait()


def put_rows(ref, at, rows):
    ref[at, 0:16, :] = rows[:, 0:128]
    ref[at, 16:32, :] = rows[:, 128:256]


def get_rows(ref, at):
    return jnp.concatenate([ref[at, 0:16, :], ref[at, 16:32, :]], axis=1)


def offer_body(which_ref, wanted_ref, kept_ref, got_ref, out_ref):
    rows = kept_ref.shape[0]
    for h in range(out_ref.shape[0] // 2):
        at = which_ref[h]
        inner = jnp.where(at < rows, at, at - rows)
        block = jnp.where(at < rows, kept_ref[inner], got_ref[inner])
        for j in range(2):
            p = 2 * h + j
            put_rows(out_ref, p, block[j * 16 : j * 16 + 16])
            out_ref[p, 32:40, :] = jnp.full((8, 128), wanted_ref[p].astype(F32), F32).astype(BF)


def pick_body(which_ref, here_ref, hub_blk_ref, blocks_ref, pieces_ref, _, out_ref, piece_ref):
    piece_ref[...] = get_rows(pieces_ref, hub_blk_ref[here_ref[0]])
    for i in range(out_ref.shape[0]):
        out_ref[i] = blocks_ref[which_ref[i]]


def spread_body(here_ref, hub_z_ref, source_ref, _, out_ref):
    chosen = source_ref[hub_z_ref[here_ref[0]]]
    for i in range(out_ref.shape[0]):
        out_ref[i] = chosen


def first_body(m_ref, feat_ref, in_ref, _, acc_ref):
    step = 128
    per_dev = feat_ref.shape[0]
    first = m_ref.shape[1] - in_ref.shape[0]

    def rows_of(i, carry):
        rows = pl.ds(pl.multiple_of(i * step, step), step)
        total = jnp.dot(m_ref[rows, 0:per_dev], feat_ref[...], preferred_element_type=F32)
        total += jnp.dot(m_ref[rows, first:], in_ref[...], preferred_element_type=F32)
        acc_ref[rows, :] = total
        return carry

    lax.fori_loop(0, per_dev // step, rows_of, 0)


def mid_body(m_ref, mine_ref, acc_ref, sum_ref, keep_ref):
    step = 128
    per_dev = acc_ref.shape[0]
    n_half = mine_ref.shape[0]

    def rows_of(i, carry):
        rows = pl.ds(pl.multiple_of(i * step, step), step)
        part = jnp.dot(m_ref[rows, 0:n_half], mine_ref[...], preferred_element_type=F32)
        sum_ref[rows, :] = acc_ref[rows, :] + part
        keep_ref[rows, :] = m_ref[rows, :]
        return carry

    lax.fori_loop(0, per_dev // step, rows_of, 0, unroll=2)


def layer_body(core_ref, acc_ref, m_ref, inv_ref, other_ref, weight_ref, cot_ref,
               out_ref, gs_out, keep_ref, send_ref, agg_s, pg_s, gs_ref, w_s, sem):
    step = 128
    per_dev, width = acc_ref.shape
    n_half = other_ref.shape[0]

    def rows_of(i, carry):
        rows = pl.ds(pl.multiple_of(i * step, step), step)
        total = acc_ref[rows, :]
        total += jnp.dot(m_ref[rows, n_half:], other_ref[...], preferred_element_type=F32)
        inv = inv_ref[rows, :]
        inv = jnp.concatenate([inv] * (width // 128), axis=1)
        agg = (total * inv).astype(BF)
        agg_s[rows, :] = agg
        pre = jnp.dot(agg, weight_ref[...], preferred_element_type=F32)
        sig = jax.nn.sigmoid(pre)
        out_ref[rows, :] = (pre * sig).astype(BF)
        slope = sig * (1.0 + pre * (1.0 - sig))
        pg = (cot_ref[rows, :].astype(F32) * slope).astype(BF)
        pg_s[rows, :] = pg
        ag = lax.dot_general(pg, weight_ref[...], NT, preferred_element_type=F32).astype(BF)
        gs_ref[rows, :] = (ag.astype(F32) * inv).astype(BF)
        return carry

    lax.fori_loop(0, per_dev // step, rows_of, 0, unroll=2)
    out_copy = pltpu.make_async_copy(gs_ref, gs_out, sem)
    out_copy.start()
    grads = gs_ref[...]
    w_s[...] = lax.dot_general(agg_s[...], pg_s[...], TN, preferred_element_type=F32)
    half = width // 2
    core = core_ref[0]
    for ref, base, part in ((send_ref, n_half, 1 - core), (keep_ref, 0, core)):
        for k in range(n_half // 256):
            cols = m_ref[:, base + k * 256 : base + (k + 1) * 256]
            piece = lax.dot_general(cols, grads, TN, preferred_element_type=F32).astype(BF)
            piece = piece.reshape(16, 16, width)
            ref[k * 16 : (k + 1) * 16, 0:16, :] = piece[:, :, 0:128]
            ref[k * 16 : (k + 1) * 16, 16:32, :] = piece[:, :, 128:256]
        wide = w_s[pl.ds(pl.multiple_of(part * half, half), half), :]
        for d in range(ref.shape[0]):
            tile = wide[(d // 2) * 8 : (d // 2) * 8 + 8, (d % 2) * 128 : (d % 2) * 128 + 128]
            ref[d, 32:40, :] = tile.astype(BF)
    out_copy.wait()


def table_body(m_ref, gs_ref, local_ref, remote_ref):
    grads = gs_ref[...]
    per_dev = local_ref.shape[0]
    for k in range(m_ref.shape[1] // 256):
        rows = slice(k * 256, (k + 1) * 256)
        piece = lax.dot_general(m_ref[:, rows], grads, TN, preferred_element_type=F32)
        if k < per_dev // 256:
            local_ref[rows, :] = piece
        else:
            remote_ref[k * 256 - per_dev : (k + 1) * 256 - per_dev, :] = piece.astype(BF)


def pair_body(keep_ref, got_ref, out_ref):
    out_ref[...] = (keep_ref[...].astype(F32) + got_ref[...].astype(F32)).astype(BF)


def sum_body(in_ref, *refs):
    out_ref = refs[-1]
    total = in_ref[0].astype(F32)
    for s in range(1, in_ref.shape[0]):
        total += in_ref[s].astype(F32)
    out_ref[...] = jnp.broadcast_to(total.astype(BF), out_ref.shape)


def gather_body(req_ref, local_ref, back_ref, out_ref):
    out_ref[...] = local_ref[...]

    def one(p, carry):
        out_ref[req_ref[p]] += back_ref[p].astype(F32)
        return carry

    lax.fori_loop(0, back_ref.shape[0], one, 0)


def finish_body(meta_ref, acc_ref, mine_ref, other_ref, out_ref, w_ref):
    out_ref[...] = acc_ref[...]
    core = meta_ref[0]
    hubs = mine_ref.shape[0] // 2
    for h in range(hubs):
        block = meta_ref[1 + h]

        @pl.when(block >= 0)
        def _():
            for ref, part in ((mine_ref, core), (other_ref, 1 - core)):
                for j in range(2):
                    rows = pl.ds(pl.multiple_of(part * HALF + j * 16, 16), 16)
                    out_ref[block, rows, :] += get_rows(ref, 2 * h + j).astype(F32)

    half = w_ref.shape[0] // 2
    for ref, part in ((mine_ref, core), (other_ref, 1 - core)):
        for d in range(ref.shape[0]):
            rows = pl.ds(pl.multiple_of(part * half + (d // 2) * 8, 8), 8)
            w_ref[rows, (d % 2) * 128 : (d % 2) * 128 + 128] = ref[d, 32:40, :].astype(F32)


def shards(features, weight, cotangent, edge_source, edge_mult, read_blocks, hub_blocks):
    per_dev, width = features.shape
    blocks_dev = per_dev // BR
    hubs = hub_blocks.shape[0]
    slots = edge_source.shape[1]
    n_blk, n_z = lax.axis_size("blk"), lax.axis_size("z")
    blk, z, core = lax.axis_index("blk"), lax.axis_index("z"), lax.axis_index("core")
    shape = jax.ShapeDtypeStruct
    exchange = functools.partial(lax.all_to_all, split_axis=0, concat_axis=0, tiled=True)
    swap = functools.partial(lax.ppermute, axis_name="core", perm=[(0, 1), (1, 0)])

    hub_device = hub_blocks // blocks_dev
    hub_local = hub_blocks % blocks_dev
    hub_blk = hub_device // (2 * n_z)
    hub_z = (hub_device // 2) % n_z
    hub_core = hub_device % 2
    device = (blk * n_z + z) * 2 + core

    own_blocks = features.reshape(blocks_dev, BR, width)
    wanted = read_blocks.reshape(-1)

    own_halves = own_blocks.reshape(blocks_dev, 2, HALF, width)
    kept = lax.dynamic_index_in_dim(own_halves, core, 1, keepdims=False)
    got = swap(lax.dynamic_index_in_dim(own_halves, 1 - core, 1, keepdims=False))
    where_half = (hub_core ^ core) * blocks_dev + hub_local
    offered = call(
        offer_body, shape((n_blk, CHUNK, 128), BF), [SMEM, SMEM, VMEM, VMEM]
    )(where_half, wanted, kept, got)
    pieces = exchange(offered, "blk")

    n_half = hubs * HALF
    core_id = core.astype(jnp.int32).reshape(1)
    groups = per_dev // GROUP
    main_rows = per_dev + n_blk * BR
    main, dense_hub, inv = call(
        build_body,
        [
            shape((groups, GROUP, main_rows), BF),
            shape((groups, GROUP, 2 * n_half), BF),
            shape((groups, GROUP, 128), F32),
        ],
        [SMEM, VMEM, VMEM],
        scratch=[pltpu.VMEM((groups, GROUP, main_rows), BF), pltpu.SemaphoreType.DMA((4,))],
        flops=10**9,
        traffic=5 << 20,
        limit=16,
        outs=[pl.BlockSpec(memory_space=pltpu.HBM), VMEM, VMEM],
    )(core_id, edge_source.reshape(groups, 1, GROUP * slots), edge_mult.reshape(groups, 1, GROUP * slots))
    main = main.reshape(per_dev, main_rows)
    dense_hub = dense_hub.reshape(per_dev, 2 * n_half)
    inv = inv.reshape(per_dev, 128)

    here = (blk // 2).astype(jnp.int32).reshape(1)
    requested = pieces[:, 32, 0].astype(jnp.int32)
    outgoing, piece = call(
        pick_body,
        [shape((n_blk, BR, width), BF), shape((16, width), BF)],
        [SMEM] * 3 + [VMEM] * 2 + [ANY],
    )(requested, here, hub_blk, own_blocks, pieces, inv)
    incoming = exchange(outgoing, "blk").reshape(-1, width)
    along = lax.all_gather(piece, "z")
    to_blk = call(spread_body, shape((n_blk, 16, width), BF), [SMEM, SMEM, VMEM, ANY])(
        here, hub_z, along, incoming
    )
    acc = call(
        first_body, shape((per_dev, width), F32), [VMEM] * 3 + [ANY], flops=10**9, traffic=6 << 20, limit=20
    )(main, features, incoming, to_blk)
    hub_mine = exchange(to_blk, "blk").reshape(-1, width)
    to_swap, acc = lax.optimization_barrier((hub_mine, acc))
    hub_other = swap(to_swap)
    acc, hub_cols = call(
        mid_body,
        [shape((per_dev, width), F32), shape(dense_hub.shape, BF)],
        [VMEM] * 3,
        flops=10**9,
        traffic=3 << 20,
        limit=12,
    )(dense_hub, hub_mine, acc)

    output, scaled, keep, send = call(
        layer_body,
        [shape((per_dev, width), BF)] * 2 + [shape((n_blk, CHUNK, 128), BF)] * 2,
        [SMEM] + [VMEM] * 6,
        scratch=[pltpu.VMEM((per_dev, width), BF)] * 3
        + [pltpu.VMEM((width, width), F32), pltpu.SemaphoreType.DMA],
        outs=[VMEM, pl.BlockSpec(memory_space=pltpu.HBM), VMEM, VMEM],
        flops=10**9,
        traffic=6 << 20,
        limit=20,
    )(core_id, acc, hub_cols, inv, hub_other, weight, cotangent)
    local_grad, remote_grad = call(
        table_body,
        [shape((per_dev, width), F32), shape((n_blk * BR, width), BF)],
        [VMEM, VMEM],
        flops=10**9,
        traffic=6 << 20,
        limit=20,
    )(main, scaled)

    chunk = shape((CHUNK, 128), BF)
    chunks = shape((n_blk, CHUNK, 128), BF)
    by_blk = exchange(call(pair_body, chunks, [VMEM, VMEM])(keep, swap(send)), "blk")
    part_sum = call(sum_body, chunk, [VMEM])(by_blk)
    remote_grad, part_sum = lax.optimization_barrier((remote_grad, part_sum))
    returned = exchange(remote_grad.reshape(n_blk, BR, width), "blk")
    full_sum = call(sum_body, chunks, [VMEM, ANY])(lax.all_gather(part_sum, "z"), returned)
    mine = exchange(full_sum, "blk")
    other = swap(mine)

    so_far = call(gather_body, shape((blocks_dev, BR, width), F32), [SMEM, VMEM, VMEM], traffic=4 << 20)(
        requested, local_grad.reshape(blocks_dev, BR, width), returned
    )
    meta = jnp.concatenate([core_id, jnp.where(hub_device == device, hub_local, -1).astype(jnp.int32)])
    feature_grad, weight_grad = call(
        finish_body,
        [shape((blocks_dev, BR, width), F32), shape((width, width), F32)],
        [SMEM] + [VMEM] * 3,
    )(meta, so_far, mine, other)
    return output, feature_grad.reshape(per_dev, width), weight_grad


def solution(mesh):
    n_blk, n_rep = mesh.devices.shape
    fine = Mesh(mesh.devices.reshape(n_blk, n_rep // 2, 2), ("blk", "z", "core"))
    axes = ("blk", "z", "core")
    rows = P(axes, None)
    in_specs = (rows, P(), rows, rows, rows, P(axes, None, None), P())
    out_specs = (rows, rows, P())
    return jax.shard_map(shards, mesh=fine, in_specs=in_specs, out_specs=out_specs, check_vma=False)
```

```python
import functools

import jax
import jax.numpy as jnp
from jax import lax
from jax.experimental import pallas as pl
from jax.experimental.pallas import tpu as pltpu
from jax.sharding import Mesh, PartitionSpec as P

BR = 64
PER_DEV = 512
HALF = BR // 2
GROUP = 16
CHUNK = 40
BF = jnp.bfloat16
F32 = jnp.float32
NT = (((1,), (1,)), ((), ()))
TN = (((0,), (0,)), ((), ()))
VMEM = pl.BlockSpec(memory_space=pltpu.VMEM)
SMEM = pl.BlockSpec(memory_space=pltpu.SMEM)
ANY = pl.BlockSpec(memory_space=pl.ANY)


def call(body, out, in_specs, scratch=(), flops=0, traffic=1 << 20, limit=8, outs=None):
    several = isinstance(out, (list, tuple))
    out_specs = outs or ([VMEM] * len(out) if several else VMEM)
    return pl.pallas_call(
        body,
        out_shape=out,
        in_specs=in_specs,
        out_specs=out_specs,
        scratch_shapes=list(scratch),
        compiler_params=pltpu.CompilerParams(vmem_limit_bytes=limit << 20),
        cost_estimate=pl.CostEstimate(flops=flops, bytes_accessed=traffic, transcendentals=0),
    )


def build_body(core_ref, idx_ref, mult_ref, main_ref, hub_ref, inv_ref, main_s, sems):
    groups, _, lanes = idx_ref.shape
    hub_cols = hub_ref.shape[2] // 128
    cols = main_ref.shape[2] // 128 + hub_cols
    first = PER_DEV // 128
    n_half = hub_cols * 64
    core = core_ref[0]
    own = (lax.broadcasted_iota(jnp.int32, (GROUP, lanes), 1) // 16) == lax.broadcasted_iota(
        jnp.int32, (GROUP, lanes), 0
    )
    low = lax.broadcasted_iota(jnp.int32, (128, lanes), 0)

    def group(g, carry):
        idx = idx_ref[g]
        row = idx - PER_DEV
        moved = PER_DEV + (((row >> 5) & 1) ^ core) * n_half + (row >> 6) * HALF + (row & (HALF - 1))
        idx = jnp.where((row >= 0) & (row < 2 * n_half), moved, idx)
        high = idx >> 7
        onehot = jnp.where(low == (idx & 127), 1.0, 0.0).astype(BF)
        mult = jnp.where(own, mult_ref[g].astype(F32), 0.0)
        inv_ref[g] = jnp.broadcast_to(1.0 / jnp.sum(mult, axis=1, keepdims=True), (GROUP, 128))
        left = jnp.concatenate([jnp.where(high == k, mult, 0.0).astype(BF) for k in range(cols)], axis=0)
        dense = lax.dot_general(left, onehot, NT, preferred_element_type=F32).astype(BF)
        for k in range(cols):
            tile = dense[k * GROUP : (k + 1) * GROUP]
            if first <= k < first + hub_cols:
                hub_ref[g, :, (k - first) * 128 : (k - first + 1) * 128] = tile
            else:
                at = k if k < first else k - hub_cols
                main_s[g, :, at * 128 : (at + 1) * 128] = tile
        return carry

    parts = sems.shape[0]
    per = groups // parts
    copies = []
    for q in range(parts):
        lax.fori_loop(q * per, (q + 1) * per, group, 0, unroll=4)
        rows = pl.ds(q * per, per)
        copies.append(pltpu.make_async_copy(main_s.at[rows], main_ref.at[rows], sems.at[q]))
        copies[-1].start()
    for copy in copies:
        copy.wait()


def put_rows(ref, at, rows):
    ref[at, 0:16, :] = rows[:, 0:128]
    ref[at, 16:32, :] = rows[:, 128:256]


def get_rows(ref, at):
    return jnp.concatenate([ref[at, 0:16, :], ref[at, 16:32, :]], axis=1)


def offer_body(which_ref, wanted_ref, kept_ref, got_ref, out_ref):
    rows = kept_ref.shape[0]
    for h in range(out_ref.shape[0] // 2):
        at = which_ref[h]
        inner = jnp.where(at < rows, at, at - rows)
        block = jnp.where(at < rows, kept_ref[inner], got_ref[inner])
        for j in range(2):
            p = 2 * h + j
            put_rows(out_ref, p, block[j * 16 : j * 16 + 16])
            out_ref[p, 32:40, :] = wanted_ref[p]


def pick_body(which_ref, here_ref, hub_blk_ref, blocks_ref, pieces_ref, _, out_ref, piece_ref):
    piece_ref[...] = get_rows(pieces_ref, hub_blk_ref[here_ref[0]])
    for i in range(out_ref.shape[0]):
        out_ref[i] = blocks_ref[which_ref[i]]


def spread_body(here_ref, hub_z_ref, source_ref, _, out_ref):
    chosen = source_ref[hub_z_ref[here_ref[0]]]
    for i in range(out_ref.shape[0]):
        out_ref[i] = chosen


def first_body(m_ref, feat_ref, in_ref, _, acc_ref):
    step = 128
    per_dev = feat_ref.shape[0]
    first = m_ref.shape[1] - in_ref.shape[0]

    def rows_of(i, carry):
        rows = pl.ds(pl.multiple_of(i * step, step), step)
        total = jnp.dot(m_ref[rows, 0:per_dev], feat_ref[...], preferred_element_type=F32)
        total += jnp.dot(m_ref[rows, first:], in_ref[...], preferred_element_type=F32)
        acc_ref[rows, :] = total
        return carry

    lax.fori_loop(0, per_dev // step, rows_of, 0)


def mid_body(m_ref, mine_ref, acc_ref, sum_ref, keep_ref):
    step = 128
    per_dev = acc_ref.shape[0]
    n_half = mine_ref.shape[0]

    def rows_of(i, carry):
        rows = pl.ds(pl.multiple_of(i * step, step), step)
        part = jnp.dot(m_ref[rows, 0:n_half], mine_ref[...], preferred_element_type=F32)
        sum_ref[rows, :] = acc_ref[rows, :] + part
        keep_ref[rows, :] = m_ref[rows, :]
        return carry

    lax.fori_loop(0, per_dev // step, rows_of, 0, unroll=2)


def layer_body(core_ref, acc_ref, m_ref, inv_ref, other_ref, weight_ref, cot_ref,
               out_ref, gs_out, keep_ref, send_ref, agg_s, pg_s, gs_ref, w_s, sem):
    step = 128
    per_dev, width = acc_ref.shape
    n_half = other_ref.shape[0]

    def rows_of(i, carry):
        rows = pl.ds(pl.multiple_of(i * step, step), step)
        total = acc_ref[rows, :]
        total += jnp.dot(m_ref[rows, n_half:], other_ref[...], preferred_element_type=F32)
        inv = inv_ref[rows, :]
        inv = jnp.concatenate([inv] * (width // 128), axis=1)
        agg = (total * inv).astype(BF)
        agg_s[rows, :] = agg
        pre = jnp.dot(agg, weight_ref[...], preferred_element_type=F32)
        sig = jax.nn.sigmoid(pre)
        out_ref[rows, :] = (pre * sig).astype(BF)
        slope = sig * (1.0 + pre * (1.0 - sig))
        pg = (cot_ref[rows, :].astype(F32) * slope).astype(BF)
        pg_s[rows, :] = pg
        ag = lax.dot_general(pg, weight_ref[...], NT, preferred_element_type=F32).astype(BF)
        gs_ref[rows, :] = (ag.astype(F32) * inv).astype(BF)
        return carry

    lax.fori_loop(0, per_dev // step, rows_of, 0, unroll=2)
    out_copy = pltpu.make_async_copy(gs_ref, gs_out, sem)
    out_copy.start()
    grads = gs_ref[...]
    w_s[...] = lax.dot_general(agg_s[...], pg_s[...], TN, preferred_element_type=F32)
    half = width // 2
    core = core_ref[0]
    for ref, base, part in ((send_ref, n_half, 1 - core), (keep_ref, 0, core)):
        for k in range(n_half // 256):
            cols = m_ref[:, base + k * 256 : base + (k + 1) * 256]
            piece = lax.dot_general(cols, grads, TN, preferred_element_type=F32).astype(BF)
            piece = piece.reshape(16, 16, width)
            ref[k * 16 : (k + 1) * 16, 0:16, :] = piece[:, :, 0:128]
            ref[k * 16 : (k + 1) * 16, 16:32, :] = piece[:, :, 128:256]
        wide = w_s[pl.ds(pl.multiple_of(part * half, half), half), :]
        for d in range(ref.shape[0]):
            tile = wide[(d // 2) * 8 : (d // 2) * 8 + 8, (d % 2) * 128 : (d % 2) * 128 + 128]
            ref[d, 32:40, :] = tile.astype(BF)
    out_copy.wait()


def table_body(m_ref, gs_ref, local_ref, remote_ref):
    grads = gs_ref[...]
    per_dev = local_ref.shape[0]
    for k in range(m_ref.shape[1] // 256):
        rows = slice(k * 256, (k + 1) * 256)
        piece = lax.dot_general(m_ref[:, rows], grads, TN, preferred_element_type=F32)
        if k < per_dev // 256:
            local_ref[rows, :] = piece
        else:
            remote_ref[k * 256 - per_dev : (k + 1) * 256 - per_dev, :] = piece.astype(BF)


def pair_body(keep_ref, got_ref, out_ref):
    out_ref[...] = (keep_ref[...].astype(F32) + got_ref[...].astype(F32)).astype(BF)


def sum_body(in_ref, *refs):
    out_ref = refs[-1]
    total = in_ref[0].astype(F32)
    for s in range(1, in_ref.shape[0]):
        total += in_ref[s].astype(F32)
    out_ref[...] = jnp.broadcast_to(total.astype(BF), out_ref.shape)


def gather_body(req_ref, local_ref, back_ref, out_ref):
    out_ref[...] = local_ref[...]

    def one(p, carry):
        out_ref[req_ref[p]] += back_ref[p].astype(F32)
        return carry

    lax.fori_loop(0, back_ref.shape[0], one, 0)


def finish_body(meta_ref, acc_ref, mine_ref, other_ref, out_ref, w_ref):
    out_ref[...] = acc_ref[...]
    core = meta_ref[0]
    hubs = mine_ref.shape[0] // 2
    for h in range(hubs):
        block = meta_ref[1 + h]

        @pl.when(block >= 0)
        def _():
            for ref, part in ((mine_ref, core), (other_ref, 1 - core)):
                for j in range(2):
                    rows = pl.ds(pl.multiple_of(part * HALF + j * 16, 16), 16)
                    out_ref[block, rows, :] += get_rows(ref, 2 * h + j).astype(F32)

    half = w_ref.shape[0] // 2
    for ref, part in ((mine_ref, core), (other_ref, 1 - core)):
        for d in range(ref.shape[0]):
            rows = pl.ds(pl.multiple_of(part * half + (d // 2) * 8, 8), 8)
            w_ref[rows, (d % 2) * 128 : (d % 2) * 128 + 128] = ref[d, 32:40, :].astype(F32)


def shards(features, weight, cotangent, edge_source, edge_mult, read_blocks, hub_blocks):
    per_dev, width = features.shape
    blocks_dev = per_dev // BR
    hubs = hub_blocks.shape[0]
    slots = edge_source.shape[1]
    n_blk, n_z = lax.axis_size("blk"), lax.axis_size("z")
    blk, z, core = lax.axis_index("blk"), lax.axis_index("z"), lax.axis_index("core")
    shape = jax.ShapeDtypeStruct
    exchange = functools.partial(lax.all_to_all, split_axis=0, concat_axis=0, tiled=True)
    swap = functools.partial(lax.ppermute, axis_name="core", perm=[(0, 1), (1, 0)])

    hub_device = hub_blocks // blocks_dev
    hub_local = hub_blocks % blocks_dev
    hub_blk = hub_device // (2 * n_z)
    hub_z = (hub_device // 2) % n_z
    hub_core = hub_device % 2
    device = (blk * n_z + z) * 2 + core

    own_blocks = features.reshape(blocks_dev, BR, width)
    wanted = jnp.broadcast_to(read_blocks.reshape(n_blk, 1, 1).astype(BF), (n_blk, 8, 128))

    own_halves = own_blocks.reshape(blocks_dev, 2, HALF, width)
    kept = lax.dynamic_index_in_dim(own_halves, core, 1, keepdims=False)
    got = swap(lax.dynamic_index_in_dim(own_halves, 1 - core, 1, keepdims=False))
    where_half = (hub_core ^ core) * blocks_dev + hub_local
    offered = call(
        offer_body, shape((n_blk, CHUNK, 128), BF), [SMEM, VMEM, VMEM, VMEM]
    )(where_half, wanted, kept, got)
    pieces = exchange(offered, "blk")

    n_half = hubs * HALF
    core_id = core.astype(jnp.int32).reshape(1)
    groups = per_dev // GROUP
    main_rows = per_dev + n_blk * BR
    main, dense_hub, inv = call(
        build_body,
        [
            shape((groups, GROUP, main_rows), BF),
            shape((groups, GROUP, 2 * n_half), BF),
            shape((groups, GROUP, 128), F32),
        ],
        [SMEM, VMEM, VMEM],
        scratch=[pltpu.VMEM((groups, GROUP, main_rows), BF), pltpu.SemaphoreType.DMA((4,))],
        flops=10**9,
        traffic=5 << 20,
        limit=16,
        outs=[pl.BlockSpec(memory_space=pltpu.HBM), VMEM, VMEM],
    )(core_id, edge_source.reshape(groups, 1, GROUP * slots), edge_mult.reshape(groups, 1, GROUP * slots))
    main = main.reshape(per_dev, main_rows)
    dense_hub = dense_hub.reshape(per_dev, 2 * n_half)
    inv = inv.reshape(per_dev, 128)

    here = (blk // 2).astype(jnp.int32).reshape(1)
    requested = pieces[:, 32, 0].astype(jnp.int32)
    outgoing, piece = call(
        pick_body,
        [shape((n_blk, BR, width), BF), shape((16, width), BF)],
        [SMEM] * 3 + [VMEM] * 2 + [ANY],
    )(requested, here, hub_blk, own_blocks, pieces, inv)
    incoming = exchange(outgoing, "blk").reshape(-1, width)
    along = lax.all_gather(piece, "z")
    to_blk = call(spread_body, shape((n_blk, 16, width), BF), [SMEM, SMEM, VMEM, ANY])(
        here, hub_z, along, incoming
    )
    acc = call(
        first_body, shape((per_dev, width), F32), [VMEM] * 3 + [ANY], flops=10**9, traffic=6 << 20, limit=20
    )(main, features, incoming, to_blk)
    hub_mine = exchange(to_blk, "blk").reshape(-1, width)
    to_swap, acc = lax.optimization_barrier((hub_mine, acc))
    hub_other = swap(to_swap)
    acc, hub_cols = call(
        mid_body,
        [shape((per_dev, width), F32), shape(dense_hub.shape, BF)],
        [VMEM] * 3,
        flops=10**9,
        traffic=3 << 20,
        limit=12,
    )(dense_hub, hub_mine, acc)

    output, scaled, keep, send = call(
        layer_body,
        [shape((per_dev, width), BF)] * 2 + [shape((n_blk, CHUNK, 128), BF)] * 2,
        [SMEM] + [VMEM] * 6,
        scratch=[pltpu.VMEM((per_dev, width), BF)] * 3
        + [pltpu.VMEM((width, width), F32), pltpu.SemaphoreType.DMA],
        outs=[VMEM, pl.BlockSpec(memory_space=pltpu.HBM), VMEM, VMEM],
        flops=10**9,
        traffic=6 << 20,
        limit=20,
    )(core_id, acc, hub_cols, inv, hub_other, weight, cotangent)
    local_grad, remote_grad = call(
        table_body,
        [shape((per_dev, width), F32), shape((n_blk * BR, width), BF)],
        [VMEM, VMEM],
        flops=10**9,
        traffic=6 << 20,
        limit=20,
    )(main, scaled)

    chunk = shape((CHUNK, 128), BF)
    chunks = shape((n_blk, CHUNK, 128), BF)
    got, local_grad, remote_grad = lax.optimization_barrier((swap(send), local_grad, remote_grad))
    by_blk = exchange(call(pair_body, chunks, [VMEM, VMEM])(keep, got), "blk")
    part_sum = call(sum_body, chunk, [VMEM])(by_blk)
    remote_grad, part_sum = lax.optimization_barrier((remote_grad, part_sum))
    returned = exchange(remote_grad.reshape(n_blk, BR, width), "blk")
    full_sum = call(sum_body, chunks, [VMEM, ANY])(lax.all_gather(part_sum, "z"), returned)
    mine = exchange(full_sum, "blk")
    other = swap(mine)

    so_far = call(gather_body, shape((blocks_dev, BR, width), F32), [SMEM, VMEM, VMEM], traffic=4 << 20)(
        requested, local_grad.reshape(blocks_dev, BR, width), returned
    )
    meta = jnp.concatenate([core_id, jnp.where(hub_device == device, hub_local, -1).astype(jnp.int32)])
    feature_grad, weight_grad = call(
        finish_body,
        [shape((blocks_dev, BR, width), F32), shape((width, width), F32)],
        [SMEM] + [VMEM] * 3,
    )(meta, so_far, mine, other)
    return output, feature_grad.reshape(per_dev, width), weight_grad


def solution(mesh):
    n_blk, n_rep = mesh.devices.shape
    fine = Mesh(mesh.devices.reshape(n_blk, n_rep // 2, 2), ("blk", "z", "core"))
    axes = ("blk", "z", "core")
    rows = P(axes, None)
    in_specs = (rows, P(), rows, rows, rows, P(axes, None, None), P())
    out_specs = (rows, rows, P())
    return jax.shard_map(shards, mesh=fine, in_specs=in_specs, out_specs=out_specs, check_vma=False)
```

```python
import functools

import jax
import jax.numpy as jnp
from jax import lax
from jax.experimental import pallas as pl
from jax.experimental.pallas import tpu as pltpu
from jax.sharding import Mesh, PartitionSpec as P

BR = 64
PER_DEV = 512
HALF = BR // 2
GROUP = 16
CHUNK = 40
BF = jnp.bfloat16
F32 = jnp.float32
NT = (((1,), (1,)), ((), ()))
TN = (((0,), (0,)), ((), ()))
VMEM = pl.BlockSpec(memory_space=pltpu.VMEM)
SMEM = pl.BlockSpec(memory_space=pltpu.SMEM)
ANY = pl.BlockSpec(memory_space=pl.ANY)


def call(body, out, in_specs, scratch=(), flops=0, traffic=1 << 20, limit=8, outs=None):
    several = isinstance(out, (list, tuple))
    out_specs = outs or ([VMEM] * len(out) if several else VMEM)
    return pl.pallas_call(
        body,
        out_shape=out,
        in_specs=in_specs,
        out_specs=out_specs,
        scratch_shapes=list(scratch),
        compiler_params=pltpu.CompilerParams(vmem_limit_bytes=limit << 20),
        cost_estimate=pl.CostEstimate(flops=flops, bytes_accessed=traffic, transcendentals=0),
    )


def build_body(core_ref, idx_ref, mult_ref, main_ref, hub_ref, inv_ref, main_s, sems):
    groups, _, lanes = idx_ref.shape
    hub_cols = hub_ref.shape[2] // 128
    cols = main_ref.shape[2] // 128 + hub_cols
    first = PER_DEV // 128
    n_half = hub_cols * 64
    core = core_ref[0]
    own = (lax.broadcasted_iota(jnp.int32, (GROUP, lanes), 1) // 16) == lax.broadcasted_iota(
        jnp.int32, (GROUP, lanes), 0
    )
    low = lax.broadcasted_iota(jnp.int32, (128, lanes), 0)

    def group(g, carry):
        idx = idx_ref[g]
        row = idx - PER_DEV
        moved = PER_DEV + (((row >> 5) & 1) ^ core) * n_half + (row >> 6) * HALF + (row & (HALF - 1))
        idx = jnp.where((row >= 0) & (row < 2 * n_half), moved, idx)
        high = idx >> 7
        onehot = jnp.where(low == (idx & 127), 1.0, 0.0).astype(BF)
        mult = jnp.where(own, mult_ref[g].astype(F32), 0.0)
        inv_ref[g] = jnp.broadcast_to(1.0 / jnp.sum(mult, axis=1, keepdims=True), (GROUP, 128))
        left = jnp.concatenate([jnp.where(high == k, mult, 0.0).astype(BF) for k in range(cols)], axis=0)
        dense = lax.dot_general(left, onehot, NT, preferred_element_type=F32).astype(BF)
        for k in range(cols):
            tile = dense[k * GROUP : (k + 1) * GROUP]
            if first <= k < first + hub_cols:
                hub_ref[g, :, (k - first) * 128 : (k - first + 1) * 128] = tile
            else:
                at = k if k < first else k - hub_cols
                main_s[g, :, at * 128 : (at + 1) * 128] = tile
        return carry

    parts = sems.shape[0]
    per = groups // parts
    copies = []
    for q in range(parts):
        lax.fori_loop(q * per, (q + 1) * per, group, 0, unroll=4)
        rows = pl.ds(q * per, per)
        copies.append(pltpu.make_async_copy(main_s.at[rows], main_ref.at[rows], sems.at[q]))
        copies[-1].start()
    for copy in copies:
        copy.wait()


def put_rows(ref, at, rows):
    ref[at, 0:16, :] = rows[:, 0:128]
    ref[at, 16:32, :] = rows[:, 128:256]


def get_rows(ref, at):
    return jnp.concatenate([ref[at, 0:16, :], ref[at, 16:32, :]], axis=1)


def offer_body(core_ref, hub_ref, wanted_ref, kept_ref, got_ref, out_ref):
    rows = kept_ref.shape[0]
    for h in range(out_ref.shape[0] // 2):
        hub = hub_ref[h]
        inner = hub & (rows - 1)
        own = ((hub // rows) & 1) == core_ref[0]
        block = jnp.where(own, kept_ref[inner], got_ref[inner])
        for j in range(2):
            p = 2 * h + j
            put_rows(out_ref, p, block[j * 16 : j * 16 + 16])
            out_ref[p, 32:40, :] = wanted_ref[p]


def pick_body(which_ref, here_ref, hub_blk_ref, blocks_ref, pieces_ref, _, out_ref, piece_ref):
    piece_ref[...] = get_rows(pieces_ref, hub_blk_ref[here_ref[0]])
    for i in range(out_ref.shape[0]):
        out_ref[i] = blocks_ref[which_ref[i]]


def spread_body(here_ref, hub_z_ref, source_ref, _, out_ref):
    chosen = source_ref[hub_z_ref[here_ref[0]]]
    for i in range(out_ref.shape[0]):
        out_ref[i] = chosen


def first_body(m_ref, feat_ref, in_ref, _, acc_ref):
    step = 128
    per_dev = feat_ref.shape[0]
    first = m_ref.shape[1] - in_ref.shape[0]

    def rows_of(i, carry):
        rows = pl.ds(pl.multiple_of(i * step, step), step)
        total = jnp.dot(m_ref[rows, 0:per_dev], feat_ref[...], preferred_element_type=F32)
        total += jnp.dot(m_ref[rows, first:], in_ref[...], preferred_element_type=F32)
        acc_ref[rows, :] = total
        return carry

    lax.fori_loop(0, per_dev // step, rows_of, 0)


def mid_body(m_ref, mine_ref, acc_ref, sum_ref, keep_ref):
    step = 128
    per_dev = acc_ref.shape[0]
    n_half = mine_ref.shape[0]

    def rows_of(i, carry):
        rows = pl.ds(pl.multiple_of(i * step, step), step)
        part = jnp.dot(m_ref[rows, 0:n_half], mine_ref[...], preferred_element_type=F32)
        sum_ref[rows, :] = acc_ref[rows, :] + part
        keep_ref[rows, :] = m_ref[rows, :]
        return carry

    lax.fori_loop(0, per_dev // step, rows_of, 0, unroll=2)


def layer_body(core_ref, acc_ref, m_ref, inv_ref, other_ref, weight_ref, cot_ref,
               out_ref, gs_out, keep_ref, send_ref, agg_s, pg_s, gs_ref, w_s, sem):
    step = 128
    per_dev, width = acc_ref.shape
    n_half = other_ref.shape[0]

    def rows_of(i, carry):
        rows = pl.ds(pl.multiple_of(i * step, step), step)
        total = acc_ref[rows, :]
        total += jnp.dot(m_ref[rows, n_half:], other_ref[...], preferred_element_type=F32)
        inv = inv_ref[rows, :]
        inv = jnp.concatenate([inv] * (width // 128), axis=1)
        agg = (total * inv).astype(BF)
        agg_s[rows, :] = agg
        pre = jnp.dot(agg, weight_ref[...], preferred_element_type=F32)
        sig = jax.nn.sigmoid(pre)
        out_ref[rows, :] = (pre * sig).astype(BF)
        slope = sig * (1.0 + pre * (1.0 - sig))
        pg = (cot_ref[rows, :].astype(F32) * slope).astype(BF)
        pg_s[rows, :] = pg
        ag = lax.dot_general(pg, weight_ref[...], NT, preferred_element_type=F32).astype(BF)
        gs_ref[rows, :] = (ag.astype(F32) * inv).astype(BF)
        return carry

    lax.fori_loop(0, per_dev // step, rows_of, 0, unroll=2)
    out_copy = pltpu.make_async_copy(gs_ref, gs_out, sem)
    out_copy.start()
    grads = gs_ref[...]
    w_s[...] = lax.dot_general(agg_s[...], pg_s[...], TN, preferred_element_type=F32)
    half = width // 2
    core = core_ref[0]
    for ref, base, part in ((send_ref, n_half, 1 - core), (keep_ref, 0, core)):
        for k in range(n_half // 256):
            cols = m_ref[:, base + k * 256 : base + (k + 1) * 256]
            piece = lax.dot_general(cols, grads, TN, preferred_element_type=F32).astype(BF)
            piece = piece.reshape(16, 16, width)
            ref[k * 16 : (k + 1) * 16, 0:16, :] = piece[:, :, 0:128]
            ref[k * 16 : (k + 1) * 16, 16:32, :] = piece[:, :, 128:256]
        wide = w_s[pl.ds(pl.multiple_of(part * half, half), half), :]
        for d in range(ref.shape[0]):
            tile = wide[(d // 2) * 8 : (d // 2) * 8 + 8, (d % 2) * 128 : (d % 2) * 128 + 128]
            ref[d, 32:40, :] = tile.astype(BF)
    out_copy.wait()


def table_body(m_ref, gs_ref, local_ref, remote_ref):
    grads = gs_ref[...]
    per_dev = local_ref.shape[0]
    for k in range(m_ref.shape[1] // 256):
        rows = slice(k * 256, (k + 1) * 256)
        piece = lax.dot_general(m_ref[:, rows], grads, TN, preferred_element_type=F32)
        if k < per_dev // 256:
            local_ref[rows, :] = piece
        else:
            remote_ref[k * 256 - per_dev : (k + 1) * 256 - per_dev, :] = piece.astype(BF)


def pair_body(keep_ref, got_ref, out_ref):
    out_ref[...] = (keep_ref[...].astype(F32) + got_ref[...].astype(F32)).astype(BF)


def sum_body(in_ref, *refs):
    out_ref = refs[-1]
    total = in_ref[0].astype(F32)
    for s in range(1, in_ref.shape[0]):
        total += in_ref[s].astype(F32)
    out_ref[...] = jnp.broadcast_to(total.astype(BF), out_ref.shape)


def gather_body(req_ref, local_ref, back_ref, out_ref):
    out_ref[...] = local_ref[...]

    def one(p, carry):
        out_ref[req_ref[p]] += back_ref[p].astype(F32)
        return carry

    lax.fori_loop(0, back_ref.shape[0], one, 0)


def finish_body(meta_ref, acc_ref, mine_ref, other_ref, out_ref, w_ref):
    out_ref[...] = acc_ref[...]
    core = meta_ref[0]
    hubs = mine_ref.shape[0] // 2
    for h in range(hubs):
        block = meta_ref[1 + h]

        @pl.when(block >= 0)
        def _():
            for ref, part in ((mine_ref, core), (other_ref, 1 - core)):
                for j in range(2):
                    rows = pl.ds(pl.multiple_of(part * HALF + j * 16, 16), 16)
                    out_ref[block, rows, :] += get_rows(ref, 2 * h + j).astype(F32)

    half = w_ref.shape[0] // 2
    for ref, part in ((mine_ref, core), (other_ref, 1 - core)):
        for d in range(ref.shape[0]):
            rows = pl.ds(pl.multiple_of(part * half + (d // 2) * 8, 8), 8)
            w_ref[rows, (d % 2) * 128 : (d % 2) * 128 + 128] = ref[d, 32:40, :].astype(F32)


def shards(features, weight, cotangent, edge_source, edge_mult, read_blocks, hub_blocks):
    per_dev, width = features.shape
    blocks_dev = per_dev // BR
    hubs = hub_blocks.shape[0]
    slots = edge_source.shape[1]
    n_blk, n_z = lax.axis_size("blk"), lax.axis_size("z")
    blk, z, core = lax.axis_index("blk"), lax.axis_index("z"), lax.axis_index("core")
    shape = jax.ShapeDtypeStruct
    exchange = functools.partial(lax.all_to_all, split_axis=0, concat_axis=0, tiled=True)
    swap = functools.partial(lax.ppermute, axis_name="core", perm=[(0, 1), (1, 0)])

    hub_device = hub_blocks // blocks_dev
    hub_local = hub_blocks % blocks_dev
    hub_blk = hub_device // (2 * n_z)
    hub_z = (hub_device // 2) % n_z
    device = (blk * n_z + z) * 2 + core

    own_blocks = features.reshape(blocks_dev, BR, width)
    wanted = jnp.broadcast_to(read_blocks.reshape(n_blk, 1, 1).astype(BF), (n_blk, 8, 128))

    own_halves = own_blocks.reshape(blocks_dev, 2, HALF, width)
    kept = lax.dynamic_index_in_dim(own_halves, core, 1, keepdims=False)
    got = swap(lax.dynamic_index_in_dim(own_halves, 1 - core, 1, keepdims=False))
    core_id = core.astype(jnp.int32).reshape(1)
    offered = call(
        offer_body, shape((n_blk, CHUNK, 128), BF), [SMEM, SMEM, VMEM, VMEM, VMEM]
    )(core_id, hub_blocks, wanted, kept, got)
    pieces = exchange(offered, "blk")

    n_half = hubs * HALF
    groups = per_dev // GROUP
    main_rows = per_dev + n_blk * BR
    main, dense_hub, inv = call(
        build_body,
        [
            shape((groups, GROUP, main_rows), BF),
            shape((groups, GROUP, 2 * n_half), BF),
            shape((groups, GROUP, 128), F32),
        ],
        [SMEM, VMEM, VMEM],
        scratch=[pltpu.VMEM((groups, GROUP, main_rows), BF), pltpu.SemaphoreType.DMA((4,))],
        flops=10**9,
        traffic=5 << 20,
        limit=16,
        outs=[pl.BlockSpec(memory_space=pltpu.HBM), VMEM, VMEM],
    )(core_id, edge_source.reshape(groups, 1, GROUP * slots), edge_mult.reshape(groups, 1, GROUP * slots))
    main = main.reshape(per_dev, main_rows)
    dense_hub = dense_hub.reshape(per_dev, 2 * n_half)
    inv = inv.reshape(per_dev, 128)

    here = (blk // 2).astype(jnp.int32).reshape(1)
    requested = pieces[:, 32, 0].astype(jnp.int32)
    outgoing, piece = call(
        pick_body,
        [shape((n_blk, BR, width), BF), shape((16, width), BF)],
        [SMEM] * 3 + [VMEM] * 2 + [ANY],
    )(requested, here, hub_blk, own_blocks, pieces, inv)
    incoming = exchange(outgoing, "blk").reshape(-1, width)
    along = lax.all_gather(piece, "z")
    to_blk = call(spread_body, shape((n_blk, 16, width), BF), [SMEM, SMEM, VMEM, ANY])(
        here, hub_z, along, incoming
    )
    acc = call(
        first_body, shape((per_dev, width), F32), [VMEM] * 3 + [ANY], flops=10**9, traffic=6 << 20, limit=20
    )(main, features, incoming, to_blk)
    hub_mine = exchange(to_blk, "blk").reshape(-1, width)
    to_swap, acc = lax.optimization_barrier((hub_mine, acc))
    hub_other = swap(to_swap)
    acc, hub_cols = call(
        mid_body,
        [shape((per_dev, width), F32), shape(dense_hub.shape, BF)],
        [VMEM] * 3,
        flops=10**9,
        traffic=3 << 20,
        limit=12,
    )(dense_hub, hub_mine, acc)

    output, scaled, keep, send = call(
        layer_body,
        [shape((per_dev, width), BF)] * 2 + [shape((n_blk, CHUNK, 128), BF)] * 2,
        [SMEM] + [VMEM] * 6,
        scratch=[pltpu.VMEM((per_dev, width), BF)] * 3
        + [pltpu.VMEM((width, width), F32), pltpu.SemaphoreType.DMA],
        outs=[VMEM, pl.BlockSpec(memory_space=pltpu.HBM), VMEM, VMEM],
        flops=10**9,
        traffic=6 << 20,
        limit=20,
    )(core_id, acc, hub_cols, inv, hub_other, weight, cotangent)
    local_grad, remote_grad = call(
        table_body,
        [shape((per_dev, width), F32), shape((n_blk * BR, width), BF)],
        [VMEM, VMEM],
        flops=10**9,
        traffic=6 << 20,
        limit=20,
    )(main, scaled)

    chunk = shape((CHUNK, 128), BF)
    chunks = shape((n_blk, CHUNK, 128), BF)
    got, local_grad, remote_grad = lax.optimization_barrier((swap(send), local_grad, remote_grad))
    by_blk = exchange(call(pair_body, chunks, [VMEM, VMEM])(keep, got), "blk")
    part_sum = call(sum_body, chunk, [VMEM])(by_blk)
    remote_grad, part_sum = lax.optimization_barrier((remote_grad, part_sum))
    returned = exchange(remote_grad.reshape(n_blk, BR, width), "blk")
    full_sum = call(sum_body, chunks, [VMEM, ANY])(lax.all_gather(part_sum, "z"), returned)
    mine = exchange(full_sum, "blk")
    other = swap(mine)

    so_far = call(gather_body, shape((blocks_dev, BR, width), F32), [SMEM, VMEM, VMEM], traffic=4 << 20)(
        requested, local_grad.reshape(blocks_dev, BR, width), returned
    )
    meta = jnp.concatenate([core_id, jnp.where(hub_device == device, hub_local, -1).astype(jnp.int32)])
    feature_grad, weight_grad = call(
        finish_body,
        [shape((blocks_dev, BR, width), F32), shape((width, width), F32)],
        [SMEM] + [VMEM] * 3,
    )(meta, so_far, mine, other)
    return output, feature_grad.reshape(per_dev, width), weight_grad


def solution(mesh):
    n_blk, n_rep = mesh.devices.shape
    fine = Mesh(mesh.devices.reshape(n_blk, n_rep // 2, 2), ("blk", "z", "core"))
    axes = ("blk", "z", "core")
    rows = P(axes, None)
    in_specs = (rows, P(), rows, rows, rows, P(axes, None, None), P())
    out_specs = (rows, rows, P())
    return jax.shard_map(shards, mesh=fine, in_specs=in_specs, out_specs=out_specs, check_vma=False)
```
